512 devices in a mesh: dp: 32 (over x, y_lo, core), mp: 16 (over y_hi, z).
Axes of the slice: x: 4, y: 8 (y_hi: 2, y_lo: 4; y = y_hi * 4 + y_lo), z: 8, core: 2. Of those that a mesh axis runs over, the one named last changes fastest.
Arguments:
- inputs: bfloat16 [2048, 8192], P('dp', 'mp'), may hold values from -6 to 6
- block_weights: bfloat16 [16, 5, 2048, 512], P('mp', None, 'dp'), may hold values from -0.125 to 0.125
- partners: int32 [16, 5], P('mp'), may hold values from 0 to 15, as said below
- code_in: bfloat16 [8192, 256], P('mp'), may hold values from -0.0625 to 0.0625
- code_out: bfloat16 [256, 16, 2048], P(None, 'mp', 'dp'), may hold values from -0.375 to 0.375
- upstream: bfloat16 [16, 2048, 2048], P('mp', None, 'dp'), may hold values from -1.5 to 1.5
Outputs:
- input_grad: bfloat16 [2048, 8192], P('dp', 'mp')
- block_grad: float32 [16, 5, 2048, 512], P('mp', None, 'dp')
- code_in_grad: float32 [8192, 256], P('mp')
- code_out_grad: float32 [256, 16, 2048], P(None, 'mp', 'dp')
The draws below stay inside these ranges and needn't reach their ends.
Inputs may be any that keep to these rules, and one draw needn't show every extreme that they name: Row i of partners lists the 5 hidden blocks i and i xor 2^k for k = 0 to 3, each once, in some order.
All inputs are finite; a program needn't handle non-finite values.
Results may differ from the reference program's by a relative error of at most 0.0059.
Values may be sent and summed in bfloat16 or wider, within the bound.
No kernel may reach another device: no remote copies, remote signals or barrier semaphores. Data moves between devices by JAX's collectives and lax.ppermute only.
A program may use at most 64 MiB of HBM per device.

```python
import jax
import jax.numpy as jnp
from jax import lax

D = 8192
NB = 16
NP = 5
R = 256
TOKENS = 2048
BR = 512
BC = 2048
N_DP = 32


def draw_partners(key, part):
    key = jax.random.fold_in(key, 7)
    scores = jax.random.randint(key, (NB, NP), 0, 1 << 20) * NP + jnp.arange(NP, dtype=jnp.int32)[None, :]
    order = jnp.argsort(scores, axis=1, stable=True).astype(jnp.int32)
    masks = jnp.where(order == 0, 0, jnp.left_shift(jnp.int32(1), jnp.maximum(order - 1, 0)))
    rows = jnp.arange(NB, dtype=jnp.int32)[:, None]
    return jnp.bitwise_xor(rows, masks).astype(jnp.int32)


def shard_levels(stream_key, shape, split, least, largest):
    level = 1.0
    for position, shards_of in split:
        heights = jax.random.uniform(jax.random.fold_in(jax.random.fold_in(stream_key, 6), position), (shards_of,), jnp.float32, least / len(split), largest / len(split))
        level = level * jnp.repeat(jnp.exp(heights), shape[position] // shards_of).reshape((-1,) + (1,) * (len(shape) - 1 - position))
    return level


def noise(key, dims, spread, reach, shards=(), kind=jnp.bfloat16):
    values = jax.random.normal(key, dims, jnp.float32) * spread
    if len(shards) > 0:
        values = shard_levels(key, dims, shards, -0.22, 0.18) * values
    return jnp.clip(values, min=-reach, max=reach).astype(kind)


def setup_inputs(seed: int = 0) -> dict:
    splits = jax.random.split(jax.random.key(seed), 7)
    inputs = noise(splits[0], (TOKENS, D), 1.0, 6.0, ((0, 32), (1, 16)))
    block_weights = noise(splits[1], (NB, NP, BC, BR), (NP * BR) ** -0.5, 0.125, ((0, 16), (2, 32)))
    partners = draw_partners(jax.random.fold_in(splits[6], 71), 0)
    code_in = noise(splits[3], (D, R), D ** -0.5, 0.0625, ((0, 16),))
    code_out = noise(splits[4], (R, NB, BC), R ** -0.5, 0.375, ((1, 16), (2, 32)))
    upstream = noise(splits[5], (NB, BC, TOKENS), 0.25, 1.5, ((0, 16), (2, 32)))
    return dict(inputs=inputs, block_weights=block_weights, partners=partners, code_in=code_in, code_out=code_out, upstream=upstream)


def gelu_slope(pre):
    return 0.5 * (1.0 + lax.erf(pre * 0.7071067811865476)) + pre * jnp.exp(-0.5 * pre * pre) * 0.3989422804014327

def reference(inputs, block_weights, partners, code_in, code_out, upstream):
    blocks_x = inputs.reshape(TOKENS, NB, BR)
    codes = jnp.dot(inputs, code_in, preferred_element_type=jnp.float32).astype(jnp.bfloat16)

    def add_row(row, hidden):
        rows_x = lax.dynamic_index_in_dim(blocks_x, row, 1, keepdims=False)
        stored = lax.dynamic_index_in_dim(block_weights, row, 0, keepdims=False)
        for slot in range(NP):
            column = partners[row, slot]
            term = jnp.dot(rows_x, stored[slot].T, preferred_element_type=jnp.float32)
            rounded = lax.optimization_barrier(term.astype(jnp.bfloat16)).astype(jnp.float32)
            term = jnp.where(column == row, term, rounded)
            hidden = hidden.at[:, column].add(term)
        return hidden
    hidden = lax.fori_loop(0, NB, add_row, jnp.zeros((TOKENS, NB, BC), jnp.float32))
    hidden = hidden + jnp.einsum('tr,rjc->tjc', codes.astype(jnp.float32), code_out.astype(jnp.float32))
    dpre = (jnp.transpose(upstream, (2, 0, 1)).astype(jnp.float32) * gelu_slope(hidden)).astype(jnp.bfloat16)
    width = BC // N_DP
    dpre_win = dpre.reshape(TOKENS, NB, N_DP, width)
    code_win = code_out.reshape(R, NB, N_DP, width)
    weight_win = block_weights.reshape(NB, NP, N_DP, width, BR)

    def window(carry, index):
        grad_acc, code_acc = carry
        slopes = lax.dynamic_index_in_dim(dpre_win, index, 2, keepdims=False)
        factor = lax.dynamic_index_in_dim(code_win, index, 2, keepdims=False)
        weights = lax.dynamic_index_in_dim(weight_win, index, 2, keepdims=False)
        back = jnp.einsum('tjc,rjc->tr', slopes.astype(jnp.float32), factor.astype(jnp.float32)).astype(jnp.bfloat16)
        picked = slopes[:, partners]
        blockwise = jnp.einsum('tisc,isck->tik', picked.astype(jnp.float32), weights.astype(jnp.float32))
        partial_grad = blockwise.reshape(TOKENS, D) + jnp.dot(back, code_in.T, preferred_element_type=jnp.float32)
        grad_acc = grad_acc + partial_grad
        code_acc = code_acc + jnp.dot(inputs.T, back, preferred_element_type=jnp.float32)
        return ((grad_acc, code_acc), None)
    start = (jnp.zeros((TOKENS, D), jnp.float32), jnp.zeros((D, R), jnp.float32))
    (grad_acc, code_acc), unused = lax.scan(window, start, jnp.arange(N_DP, dtype=jnp.int32))
    input_grad = grad_acc.astype(jnp.bfloat16)

    def row_grad(row):
        picked = dpre[:, partners[row]]
        rows_x = lax.dynamic_index_in_dim(blocks_x, row, 1, keepdims=False)
        return jnp.einsum('tsc,tk->sck', picked.astype(jnp.float32), rows_x.astype(jnp.float32))
    block_grad = lax.map(row_grad, jnp.arange(NB, dtype=jnp.int32))
    code_out_grad = jnp.einsum('tr,tjc->rjc', codes.astype(jnp.float32), dpre.astype(jnp.float32))
    return (input_grad, block_grad, code_acc, code_out_grad)
```

```python
import jax
import jax.numpy as jnp
from jax import lax
from jax.sharding import Mesh, PartitionSpec as P

F32 = jnp.float32
BF16 = jnp.bfloat16
X, Y, C, H, Z = 4, 4, 2, 2, 8
MASKS = (0, 1, 2, 4, 8)


def gelu_slope(pre):
    return (
        0.5 * (1.0 + lax.erf(pre * 0.7071067811865476))
        + pre * jnp.exp(-0.5 * pre * pre) * 0.3989422804014327
    )


def dot(a, b, lhs, rhs):
    return lax.dot_general(a, b, (((lhs,), (rhs,)), ((), ())), preferred_element_type=F32)


def exchange(block, axes):
    return lax.all_to_all(block, axes, 0, 0, tiled=True)


def spread(block, axes, count):
    return exchange(jnp.broadcast_to(block[None], (count,) + block.shape), axes)


def swap_core(block):
    return lax.ppermute(block, "c", [(0, 1), (1, 0)])


def from_partner(block, mask):
    if mask == 8:
        return lax.ppermute(block, "h", [(0, 1), (1, 0)])
    return lax.ppermute(block, "z", [(k, k ^ mask) for k in range(Z)])


def body(inputs, block_weights, partners, code_in, code_out, upstream):
    core = lax.axis_index("c")
    row = lax.axis_index("h") * Z + lax.axis_index("z")
    own = inputs.shape[0]
    width = block_weights.shape[2]
    rows = block_weights.shape[3]
    slots = len(MASKS)
    rank = code_in.shape[1]
    peers = X * Y
    tokens = peers * own

    targets = jnp.bitwise_xor(row, jnp.array(MASKS, jnp.int32))
    select = partners[0][None, :] == targets[:, None]
    slot_of = jnp.argmax(select, axis=1)
    kind_of = jnp.argmax(select, axis=0)

    near = spread(inputs, ("y",), Y).reshape(Y * own, rows)
    tile = spread(near, ("x",), X).reshape(tokens, rows)

    factor = code_out[:, 0, :].T
    half = width // 2
    packed = jnp.concatenate([factor[:half], factor[half:]], axis=1)
    mine = jnp.concatenate([block_weights[0].reshape(slots * width, rows), packed], axis=0)
    other = swap_core(mine)
    last = other[slots * width :]
    factor = jnp.concatenate([factor, last[:, :rank], last[:, rank:]], axis=0)
    weights = jnp.concatenate(
        [block_weights[0], other[: slots * width].reshape(slots, width, rows)], axis=1
    )
    weights = weights[slot_of]
    columns = 2 * width

    codes = dot(inputs, code_in, 1, 0)
    for mask in MASKS[1:]:
        codes = codes + from_partner(codes, mask)
    codes = codes.astype(BF16)

    sent = upstream[0].T.reshape(own, peers, columns).transpose(1, 0, 2)
    sent = jnp.concatenate(
        [sent, jnp.broadcast_to(codes[None], (peers, own, rank))], axis=2
    )
    sent = exchange(sent, ("x", "y")).reshape(tokens, columns + rank)
    slopes_in = sent[:, :columns].astype(F32)
    slopes_in = jnp.where(core == 0, slopes_in, jnp.roll(slopes_in, width, axis=1))
    codes = sent[:, columns:]

    products = dot(tile, weights.reshape(slots * columns, rows), 1, 1)
    hidden = products[:, :columns]
    for kind in (3, 4, 2, 1):
        term = products[:, kind * columns : (kind + 1) * columns].astype(BF16)
        hidden = hidden + from_partner(term, MASKS[kind]).astype(F32)
    hidden = hidden + dot(codes, factor, 1, 1)
    dpre = (slopes_in * gelu_slope(hidden)).astype(BF16)

    back = dot(dpre, factor, 1, 0).astype(BF16).reshape(peers, own, rank)
    back = exchange(back, ("x", "y")).astype(F32).sum(0).astype(BF16)
    back = spread(back, ("h", "z"), H * Z).astype(F32).sum(0)
    back = back.astype(BF16)

    kinds = [dpre] + [from_partner(dpre, mask) for mask in MASKS[1:]]
    stacked = jnp.concatenate(kinds, axis=1)

    partial = dot(stacked, weights.reshape(slots * columns, rows), 1, 0)
    partial = partial.astype(BF16).reshape(X, Y * own, rows)
    partial = exchange(partial, ("x",)).astype(F32).sum(0).astype(BF16)
    partial = exchange(partial.reshape(Y, own, rows), ("y",)).astype(F32).sum(0)
    input_grad = (partial + dot(back, code_in, 1, 1)).astype(BF16)

    block_grad = dot(stacked, tile, 0, 0).reshape(slots, columns, rows)[kind_of]
    factor_grad = dot(dpre, codes, 0, 0)
    away = factor_grad[width:]
    away = jnp.concatenate([away[:half], away[half:]], axis=1)
    away = jnp.concatenate([block_grad[:, width:].reshape(slots * width, rows), away], axis=0)
    came = swap_core(away)
    block_grad = block_grad[:, :width] + came[: slots * width].reshape(slots, width, rows)
    last = came[slots * width :]
    factor_grad = factor_grad[:width] + jnp.concatenate([last[:, :rank], last[:, rank:]], axis=0)

    back = spread(back, ("y",), Y).reshape(Y * own, rank)
    back = spread(back, ("x",), X).reshape(tokens, rank)
    code_in_grad = dot(tile, back, 0, 0)
    code_in_grad = code_in_grad + swap_core(code_in_grad)

    return (input_grad, block_grad[None], code_in_grad, factor_grad.T[:, None, :])


def solution(mesh):
    fine = Mesh(mesh.devices.reshape(X, Y, C, H, Z), ("x", "y", "c", "h", "z"))
    dp, mp = ("x", "y", "c"), ("h", "z")
    in_specs = (
        P(dp, mp),
        P(mp, None, dp, None),
        P(mp, None),
        P(mp, None),
        P(None, mp, dp),
        P(mp, None, dp),
    )
    out_specs = (P(dp, mp), P(mp, None, dp, None), P(mp, None), P(None, mp, dp))
    return jax.shard_map(body, mesh=fine, in_specs=in_specs, out_specs=out_specs, check_vma=False)
```

```python
import jax
import jax.numpy as jnp
from jax import lax
from jax.experimental import pallas as pl
from jax.experimental.pallas import tpu as pltpu
from jax.sharding import Mesh, PartitionSpec as P

F32 = jnp.float32
BF16 = jnp.bfloat16
X, Y, C, H, Z = 4, 4, 2, 2, 8
MASKS = (0, 1, 2, 4, 8)
SLOTS = 5
OWN = 64
ROWS = 512
RANK = 256
PEERS = X * Y
TOKENS = PEERS * OWN
COLS = 2 * OWN
STEP = 256


def gelu_slope(pre):
    return (
        0.5 * (1.0 + lax.erf(pre * 0.7071067811865476))
        + pre * jnp.exp(-0.5 * pre * pre) * 0.3989422804014327
    )


def dot(a, b, lhs, rhs):
    return lax.dot_general(a, b, (((lhs,), (rhs,)), ((), ())), preferred_element_type=F32)


def exchange(block, axes):
    return lax.all_to_all(block, axes, 0, 0, tiled=True)


def spread(block, axes, count):
    return exchange(jnp.broadcast_to(block[None], (count,) + block.shape), axes)


def swap_core(block):
    return lax.ppermute(block, "c", [(0, 1), (1, 0)])


def from_partner(block, mask):
    if mask == 8:
        return lax.ppermute(block, "h", [(0, 1), (1, 0)])
    return lax.ppermute(block, "z", [(k, k ^ mask) for k in range(Z)])


def after(value, *others):
    return lax.optimization_barrier((value, *others))[0]


SMEM = pl.BlockSpec(memory_space=pltpu.SMEM)
VMEM = pl.BlockSpec(memory_space=pltpu.VMEM)


def call(kernel, ins, outs, flops, *args):
    size = sum(a.size * a.dtype.itemsize for a in args)
    size += sum(int(jnp.dtype(o.dtype).itemsize) * o.size for o in outs)
    return pl.pallas_call(
        kernel,
        out_shape=outs,
        in_specs=ins,
        out_specs=[VMEM] * len(outs),
        cost_estimate=pl.CostEstimate(flops=flops, bytes_accessed=size, transcendentals=0),
        compiler_params=pltpu.CompilerParams(vmem_limit_bytes=10 * 1024 * 1024),
    )(*args)


def shape(dims, dtype):
    return jax.ShapeDtypeStruct(dims, dtype)


def all_weights(slot_ref, mine_ref, other_ref):
    parts = []
    for kind in range(SLOTS):
        slot = slot_ref[kind]
        parts.append(mine_ref[slot])
        parts.append(other_ref[pl.ds(pl.multiple_of(slot * OWN, OWN), OWN), :])
    return jnp.concatenate(parts, axis=0)


def all_factor(factor_ref, other_ref):
    last = other_ref[SLOTS * OWN :, :]
    return jnp.concatenate([factor_ref[...], last[:, :RANK], last[:, RANK:]], axis=0)


def forward_kernel(slot_ref, tile_ref, mine_ref, other_ref, *outs):
    weights = all_weights(slot_ref, mine_ref, other_ref)
    for part in range(X):
        rows = pl.ds(part * STEP, STEP)
        products = dot(tile_ref[rows, :], weights, 1, 1)
        outs[0][rows, :] = products[:, :COLS]
        for kind in range(1, SLOTS):
            outs[kind][rows, :] = products[:, kind * COLS : (kind + 1) * COLS].astype(BF16)


def hidden_kernel(core_ref, hidden_ref, a, b, c, d, sent_ref, factor_ref, other_ref, dpre_ref, back_ref):
    factor = all_factor(factor_ref, other_ref)
    core = core_ref[0]
    for part in range(X):
        rows = pl.ds(part * STEP, STEP)
        hidden = hidden_ref[rows, :]
        for arrived in (a, b, c, d):
            hidden = hidden + arrived[rows, :].astype(F32)
        hidden = hidden + dot(sent_ref[rows, COLS:], factor, 1, 1)
        up = sent_ref[rows, :COLS].astype(F32)
        up = jnp.where(core == 0, up, pltpu.roll(up, OWN, 1))
        dpre = (up * gelu_slope(hidden)).astype(BF16)
        dpre_ref[rows, :] = dpre
        back_ref[rows, :] = dot(dpre, factor, 1, 0).astype(BF16)


def input_kernel(slot_ref, a, b, c, d, e, mine_ref, other_ref, out_ref):
    weights = all_weights(slot_ref, mine_ref, other_ref)
    for part in range(X):
        rows = pl.ds(part * STEP, STEP)
        stacked = jnp.concatenate([k[rows, :] for k in (a, b, c, d, e)], axis=1)
        out_ref[rows, :] = dot(stacked, weights, 1, 0).astype(BF16)


def weight_kernel(slot_ref, a, b, c, d, e, tile_ref, sent_ref, keep_ref, away_ref, factor_ref):
    for kind, grads in enumerate((a, b, c, d, e)):
        slot = slot_ref[kind]
        full = dot(grads[...], tile_ref[...], 0, 0)
        keep_ref[slot] = full[:OWN]
        away_ref[pl.ds(pl.multiple_of(slot * OWN, OWN), OWN), :] = full[OWN:]
    full = dot(a[...], sent_ref[:, COLS:], 0, 0)
    factor_ref[...] = full[:OWN]
    away_ref[SLOTS * OWN :, :RANK] = full[OWN : OWN + OWN // 2]
    away_ref[SLOTS * OWN :, RANK:] = full[OWN + OWN // 2 :]


def code_kernel(tile_ref, back_ref, out_ref):
    out_ref[...] = dot(tile_ref[...], back_ref[...], 0, 0)


def body(inputs, block_weights, partners, code_in, code_out, upstream):
    core = lax.axis_index("c").reshape(1)
    row = lax.axis_index("h") * Z + lax.axis_index("z")

    targets = jnp.bitwise_xor(row, jnp.array(MASKS, jnp.int32))
    slots = jnp.sum(
        jnp.where(partners[0][None, :] == targets[:, None], jnp.arange(SLOTS)[None, :], 0), axis=1
    ).astype(jnp.int32)

    tile = spread(inputs, ("x", "y"), PEERS).reshape(TOKENS, ROWS)

    factor = code_out[:, 0, :].T
    packed = jnp.concatenate([factor[: OWN // 2], factor[OWN // 2 :]], axis=1)
    mine = block_weights[0]
    other = swap_core(jnp.concatenate([mine.reshape(SLOTS * OWN, ROWS), packed], axis=0))

    codes = dot(inputs, code_in, 1, 0)
    for mask in (1, 2):
        codes = codes + from_partner(codes, mask)
    codes = after(codes, other)
    codes = codes + from_partner(codes, 4)

    tall = [shape((TOKENS, COLS), BF16)] * 4
    hidden, *terms = call(
        forward_kernel, [SMEM] + [VMEM] * 3, [shape((TOKENS, COLS), F32)] + tall,
        2 * TOKENS * COLS * SLOTS * ROWS, slots, tile, mine, other,
    )
    codes = after(codes, hidden)
    codes = (codes + from_partner(codes, 8)).astype(BF16)
    arrived = [from_partner(term, mask) for term, mask in zip(terms, MASKS[1:])]

    sent = upstream[0].T.reshape(OWN, PEERS, COLS).transpose(1, 0, 2)
    sent = jnp.concatenate([sent, jnp.broadcast_to(codes[None], (PEERS, OWN, RANK))], axis=2)
    sent = exchange(sent, ("x", "y")).reshape(TOKENS, COLS + RANK)
    dpre, back = call(
        hidden_kernel, [SMEM] + [VMEM] * 8,
        [shape((TOKENS, COLS), BF16), shape((TOKENS, RANK), BF16)],
        4 * TOKENS * COLS * RANK, core, hidden, *arrived, sent, factor, other,
    )
    kinds = [dpre] + [from_partner(dpre, mask) for mask in MASKS[1:]]

    back = exchange(back.reshape(PEERS * H, OWN // H, RANK), ("x", "y", "h")).astype(F32).sum(0)

    (partial,) = call(
        input_kernel, [SMEM] + [VMEM] * 7, [shape((TOKENS, ROWS), BF16)],
        2 * TOKENS * COLS * SLOTS * ROWS, slots, *kinds, mine, other,
    )
    back = after(back, partial)
    partial = exchange(partial.reshape(X, Y * OWN, ROWS), ("x",)).astype(F32).sum(0).astype(BF16)
    for mask in MASKS[1:4]:
        back = back + from_partner(back, mask)
    back = spread(back.astype(BF16), ("x", "y", "h"), PEERS * H).reshape(TOKENS, RANK)
    partial = after(partial, back)
    partial = exchange(partial.reshape(Y, OWN, ROWS), ("y",))
    place = (lax.axis_index("x") * Y + lax.axis_index("y")) * OWN
    own_back = lax.dynamic_slice_in_dim(back, place, OWN, 0)
    input_grad = partial.astype(F32).sum(0) + dot(own_back, code_in, 1, 1)
    input_grad = input_grad.astype(BF16)

    keep, away, factor_grad = call(
        weight_kernel, [SMEM] + [VMEM] * 7,
        [shape((SLOTS, OWN, ROWS), F32), shape((SLOTS * OWN + OWN // 2, ROWS), F32), shape((OWN, RANK), F32)],
        2 * TOKENS * COLS * (SLOTS * ROWS + RANK), slots, *kinds, tile, sent,
    )
    came = swap_core(away)
    block_grad = keep + came[: SLOTS * OWN].reshape(SLOTS, OWN, ROWS)
    last = came[SLOTS * OWN :]
    factor_grad = factor_grad + jnp.concatenate([last[:, :RANK], last[:, RANK:]], axis=0)

    (code_in_grad,) = call(
        code_kernel, [VMEM] * 2, [shape((ROWS, RANK), F32)], 2 * TOKENS * ROWS * RANK, tile, back
    )
    code_in_grad = code_in_grad + swap_core(code_in_grad)

    return (input_grad, block_grad[None], code_in_grad, factor_grad.T[:, None, :])


def solution(mesh):
    fine = Mesh(mesh.devices.reshape(X, Y, C, H, Z), ("x", "y", "c", "h", "z"))
    dp, mp = ("x", "y", "c"), ("h", "z")
    in_specs = (
        P(dp, mp),
        P(mp, None, dp, None),
        P(mp, None),
        P(mp, None),
        P(None, mp, dp),
        P(mp, None, dp),
    )
    out_specs = (P(dp, mp), P(mp, None, dp, None), P(mp, None), P(None, mp, dp))
    return jax.shard_map(body, mesh=fine, in_specs=in_specs, out_specs=out_specs, check_vma=False)
```

```python
import jax
import jax.numpy as jnp
from jax import lax
from jax.experimental import pallas as pl
from jax.experimental.pallas import tpu as pltpu
from jax.sharding import Mesh, PartitionSpec as P

F32 = jnp.float32
BF16 = jnp.bfloat16
X, Y, C, H, Z = 4, 4, 2, 2, 8
MASKS = (0, 1, 2, 4, 8)
SLOTS = 5
OWN = 64
ROWS = 512
RANK = 256
PEERS = X * Y
TOKENS = PEERS * OWN
COLS = 2 * OWN
STEP = 256


def gelu_slope(pre):
    return (
        0.5 * (1.0 + lax.erf(pre * 0.7071067811865476))
        + pre * jnp.exp(-0.5 * pre * pre) * 0.3989422804014327
    )


def dot(a, b, lhs, rhs):
    return lax.dot_general(a, b, (((lhs,), (rhs,)), ((), ())), preferred_element_type=F32)


def exchange(block, axes):
    return lax.all_to_all(block, axes, 0, 0, tiled=True)


def spread(block, axes, count):
    return exchange(jnp.broadcast_to(block[None], (count,) + block.shape), axes)


def swap_core(block):
    return lax.ppermute(block, "c", [(0, 1), (1, 0)])


def from_partner(block, mask):
    if mask == 8:
        return lax.ppermute(block, "h", [(0, 1), (1, 0)])
    return lax.ppermute(block, "z", [(k, k ^ mask) for k in range(Z)])


def to_x(block, shift):
    return lax.ppermute(block, "x", [(k, (k + shift) % X) for k in range(X)])


def after(value, *others):
    return lax.optimization_barrier((value, *others))[0]


SMEM = pl.BlockSpec(memory_space=pltpu.SMEM)
VMEM = pl.BlockSpec(memory_space=pltpu.VMEM)


def call(kernel, ins, outs, flops, *args):
    size = sum(a.size * a.dtype.itemsize for a in args)
    size += sum(int(jnp.dtype(o.dtype).itemsize) * o.size for o in outs)
    return pl.pallas_call(
        kernel,
        out_shape=outs,
        in_specs=ins,
        out_specs=[VMEM] * len(outs),
        cost_estimate=pl.CostEstimate(flops=flops, bytes_accessed=size, transcendentals=0),
        compiler_params=pltpu.CompilerParams(vmem_limit_bytes=10 * 1024 * 1024),
    )(*args)


def shape(dims, dtype):
    return jax.ShapeDtypeStruct(dims, dtype)


def all_weights(slot_ref, mine_ref, other_ref):
    parts = []
    for kind in range(SLOTS):
        slot = slot_ref[kind]
        parts.append(mine_ref[slot])
        parts.append(other_ref[pl.ds(pl.multiple_of(slot * OWN, OWN), OWN), :])
    return jnp.concatenate(parts, axis=0)


def all_factor(factor_ref, other_ref):
    last = other_ref[SLOTS * OWN :, :]
    return jnp.concatenate([factor_ref[...], last[:, :RANK], last[:, RANK:]], axis=0)


def place_of(x, shift):
    return pl.ds(pl.multiple_of(lax.rem(x + shift, X) * STEP, STEP), STEP)


def forward_kernel(slot_ref, x_ref, t0, t1, t2, t3, mine_ref, other_ref, tile_ref, *outs):
    weights = all_weights(slot_ref, mine_ref, other_ref)
    for shift, part in enumerate((t0, t1, t2, t3)):
        rows = place_of(x_ref[0], X - shift)
        tile_ref[rows, :] = part[...]
        products = dot(part[...], weights, 1, 1)
        outs[0][rows, :] = products[:, :COLS]
        for kind in range(1, SLOTS):
            outs[kind][rows, :] = products[:, kind * COLS : (kind + 1) * COLS].astype(BF16)


def low_kernel(hidden_ref, sent_ref, factor_ref, other_ref, out_ref):
    factor = all_factor(factor_ref, other_ref)
    for part in range(X):
        rows = pl.ds(part * STEP, STEP)
        out_ref[rows, :] = hidden_ref[rows, :] + dot(sent_ref[rows, COLS:], factor, 1, 1)


def hidden_kernel(core_ref, hidden_ref, a, b, c, d, sent_ref, factor_ref, other_ref, dpre_ref, back_ref):
    factor = all_factor(factor_ref, other_ref)
    core = core_ref[0]
    for part in range(X):
        rows = pl.ds(part * STEP, STEP)
        hidden = hidden_ref[rows, :]
        for arrived in (a, b, c, d):
            hidden = hidden + arrived[rows, :].astype(F32)
        up = sent_ref[rows, :COLS].astype(F32)
        up = jnp.where(core == 0, up, pltpu.roll(up, OWN, 1))
        dpre = (up * gelu_slope(hidden)).astype(BF16)
        dpre_ref[rows, :] = dpre
        back_ref[rows, :] = dot(dpre, factor, 1, 0).astype(BF16)


def input_kernel(slot_ref, x_ref, a, b, c, d, e, mine_ref, other_ref, own_ref, *outs):
    weights = all_weights(slot_ref, mine_ref, other_ref)
    for shift in (2, 1, 3, 0):
        rows = place_of(x_ref[0], shift)
        stacked = jnp.concatenate([k[rows, :] for k in (a, b, c, d, e)], axis=1)
        result = dot(stacked, weights, 1, 0)
        if shift == 0:
            own_ref[...] = result
        else:
            outs[shift - 1][...] = result.astype(BF16)


def weight_kernel(slot_ref, a, b, c, d, e, tile_ref, sent_ref, keep_ref, away_ref, factor_ref):
    for kind, grads in enumerate((a, b, c, d, e)):
        slot = slot_ref[kind]
        full = dot(grads[...], tile_ref[...], 0, 0)
        keep_ref[slot] = full[:OWN]
        away_ref[pl.ds(pl.multiple_of(slot * OWN, OWN), OWN), :] = full[OWN:]
    full = dot(a[...], sent_ref[:, COLS:], 0, 0)
    factor_ref[...] = full[:OWN]
    away_ref[SLOTS * OWN :, :RANK] = full[OWN : OWN + OWN // 2]
    away_ref[SLOTS * OWN :, RANK:] = full[OWN + OWN // 2 :]


def code_kernel(tile_ref, back_ref, out_ref):
    out_ref[...] = dot(tile_ref[...], back_ref[...], 0, 0)


def body(inputs, block_weights, partners, code_in, code_out, upstream):
    core = lax.axis_index("c").reshape(1)
    place = lax.axis_index("x").reshape(1)
    row = lax.axis_index("h") * Z + lax.axis_index("z")
    own = (lax.axis_index("x") * Y + lax.axis_index("y")) * OWN
    inputs, core, place, row, own = lax.optimization_barrier((inputs, core, place, row, own))

    targets = jnp.bitwise_xor(row, jnp.array(MASKS, jnp.int32))
    slots = jnp.sum(
        jnp.where(partners[0][None, :] == targets[:, None], jnp.arange(SLOTS)[None, :], 0), axis=1
    ).astype(jnp.int32)

    factor = code_out[:, 0, :].T
    packed = jnp.concatenate([factor[: OWN // 2], factor[OWN // 2 :]], axis=1)
    mine = block_weights[0]
    other = swap_core(jnp.concatenate([mine.reshape(SLOTS * OWN, ROWS), packed], axis=0))

    near = spread(inputs, ("y",), Y).reshape(Y * OWN, ROWS)
    near = after(near, other)
    far = [to_x(near, shift) for shift in range(1, X)]

    codes = dot(inputs, code_in, 1, 0).astype(BF16)
    codes = spread(after(codes, near), ("h", "z"), H * Z)
    codes = codes.astype(F32).sum(0).astype(BF16)
    near = after(near, codes)

    tall = [shape((TOKENS, COLS), BF16)] * 4
    tile, hidden, *terms = call(
        forward_kernel, [SMEM] * 2 + [VMEM] * 6,
        [shape((TOKENS, ROWS), BF16), shape((TOKENS, COLS), F32)] + tall,
        2 * TOKENS * COLS * SLOTS * ROWS, slots, place, near, *far, mine, other,
    )
    arrived = [from_partner(term, mask) for term, mask in zip(terms, MASKS[1:])]

    sent = upstream[0].T.reshape(OWN, PEERS, COLS).transpose(1, 0, 2)
    sent = jnp.concatenate([sent, jnp.broadcast_to(codes[None], (PEERS, OWN, RANK))], axis=2)
    sent = exchange(after(sent, hidden), ("x", "y")).reshape(TOKENS, COLS + RANK)
    (hidden,) = call(
        low_kernel, [VMEM] * 4, [shape((TOKENS, COLS), F32)],
        2 * TOKENS * COLS * RANK, hidden, sent, factor, other,
    )
    arrived = lax.optimization_barrier((hidden, *arrived))[1:]
    dpre, back = call(
        hidden_kernel, [SMEM] + [VMEM] * 8,
        [shape((TOKENS, COLS), BF16), shape((TOKENS, RANK), BF16)],
        2 * TOKENS * COLS * RANK, core, hidden, *arrived, sent, factor, other,
    )
    kinds = [dpre] + [from_partner(dpre, mask) for mask in MASKS[1:]]

    back = exchange(back.reshape(PEERS * H, OWN // H, RANK), ("x", "y", "h")).astype(F32).sum(0)

    back = back.astype(BF16)
    back = spread(back, ("z",), Z).astype(F32).sum(0).astype(BF16)
    kinds = lax.optimization_barrier((back, *kinds))[1:]
    back = spread(back, ("x", "y", "h"), PEERS * H).reshape(TOKENS, RANK)

    partial, *away = call(
        input_kernel, [SMEM] * 2 + [VMEM] * 7,
        [shape((STEP, ROWS), F32)] + [shape((STEP, ROWS), BF16)] * 3,
        2 * TOKENS * COLS * SLOTS * ROWS, slots, place, *kinds, mine, other,
    )
    came = [to_x(part, shift) for shift, part in enumerate(away, 1)]
    kinds = lax.optimization_barrier((*kinds, *came))[:SLOTS]
    for part in came:
        partial = partial + part.astype(F32)
    partial = after(partial, back)
    partial = exchange(partial.astype(BF16).reshape(Y, OWN, ROWS), ("y",))
    own_back = lax.dynamic_slice_in_dim(back, own, OWN, 0)
    input_grad = partial.astype(F32).sum(0) + dot(own_back, code_in, 1, 1)
    input_grad = input_grad.astype(BF16)

    keep, away, factor_grad = call(
        weight_kernel, [SMEM] + [VMEM] * 7,
        [shape((SLOTS, OWN, ROWS), F32), shape((SLOTS * OWN + OWN // 2, ROWS), F32), shape((OWN, RANK), F32)],
        2 * TOKENS * COLS * (SLOTS * ROWS + RANK), slots, *kinds, tile, sent,
    )
    came = swap_core(away)
    block_grad = keep + came[: SLOTS * OWN].reshape(SLOTS, OWN, ROWS)
    last = came[SLOTS * OWN :]
    factor_grad = factor_grad + jnp.concatenate([last[:, :RANK], last[:, RANK:]], axis=0)

    (code_in_grad,) = call(
        code_kernel, [VMEM] * 2, [shape((ROWS, RANK), F32)], 2 * TOKENS * ROWS * RANK, tile, back
    )
    code_in_grad = code_in_grad + swap_core(code_in_grad)

    return (input_grad, block_grad[None], code_in_grad, factor_grad.T[:, None, :])


def solution(mesh):
    fine = Mesh(mesh.devices.reshape(X, Y, C, H, Z), ("x", "y", "c", "h", "z"))
    dp, mp = ("x", "y", "c"), ("h", "z")
    in_specs = (
        P(dp, mp),
        P(mp, None, dp, None),
        P(mp, None),
        P(mp, None),
        P(None, mp, dp),
        P(mp, None, dp),
    )
    out_specs = (P(dp, mp), P(mp, None, dp, None), P(mp, None), P(None, mp, dp))
    return jax.shard_map(body, mesh=fine, in_specs=in_specs, out_specs=out_specs, check_vma=False)
```

```python
import jax
import jax.numpy as jnp
from jax import lax
from jax.experimental import pallas as pl
from jax.experimental.pallas import tpu as pltpu
from jax.sharding import Mesh, PartitionSpec as P

F32 = jnp.float32
BF16 = jnp.bfloat16
X, Y, C, H, Z = 4, 4, 2, 2, 8
MASKS = (0, 1, 2, 4, 8)
SLOTS = 5
OWN = 64
ROWS = 512
RANK = 256
PEERS = X * Y
TOKENS = PEERS * OWN
COLS = 2 * OWN
STEP = 256


def gelu_slope(pre):
    return (
        0.5 * (1.0 + lax.erf(pre * 0.7071067811865476))
        + pre * jnp.exp(-0.5 * pre * pre) * 0.3989422804014327
    )


def dot(a, b, lhs, rhs):
    return lax.dot_general(a, b, (((lhs,), (rhs,)), ((), ())), preferred_element_type=F32)


def exchange(block, axes):
    return lax.all_to_all(block, axes, 0, 0, tiled=True)


def spread(block, axes, count):
    return exchange(jnp.broadcast_to(block[None], (count,) + block.shape), axes)


def swap_core(block):
    return lax.ppermute(block, "c", [(0, 1), (1, 0)])


def from_partner(block, mask):
    if mask == 8:
        return lax.ppermute(block, "h", [(0, 1), (1, 0)])
    return lax.ppermute(block, "z", [(k, k ^ mask) for k in range(Z)])


def to_x(block, shift):
    return lax.ppermute(block, "x", [(k, (k + shift) % X) for k in range(X)])


def after(value, *others):
    return lax.optimization_barrier((value, *others))[0]


SMEM = pl.BlockSpec(memory_space=pltpu.SMEM)
VMEM = pl.BlockSpec(memory_space=pltpu.VMEM)


def call(kernel, ins, outs, flops, *args):
    size = sum(a.size * a.dtype.itemsize for a in args)
    size += sum(int(jnp.dtype(o.dtype).itemsize) * o.size for o in outs)
    return pl.pallas_call(
        kernel,
        out_shape=outs,
        in_specs=ins,
        out_specs=[VMEM] * len(outs),
        cost_estimate=pl.CostEstimate(flops=flops, bytes_accessed=size, transcendentals=0),
        compiler_params=pltpu.CompilerParams(vmem_limit_bytes=10 * 1024 * 1024),
    )(*args)


def shape(dims, dtype):
    return jax.ShapeDtypeStruct(dims, dtype)


def all_weights(slot_ref, mine_ref, other_ref):
    parts = []
    for kind in range(SLOTS):
        slot = slot_ref[kind]
        parts.append(mine_ref[slot])
        parts.append(other_ref[pl.ds(pl.multiple_of(slot * OWN, OWN), OWN), :])
    return jnp.concatenate(parts, axis=0)


def all_factor(factor_ref, other_ref):
    last = other_ref[SLOTS * OWN :, :]
    return jnp.concatenate([factor_ref[...], last[:, :RANK], last[:, RANK:]], axis=0)


def place_of(x, shift):
    return pl.ds(pl.multiple_of(lax.rem(x + shift, X) * STEP, STEP), STEP)


def forward_kernel(slot_ref, x_ref, t0, t1, t2, t3, mine_ref, other_ref, *outs):
    weights = all_weights(slot_ref, mine_ref, other_ref)
    for shift, part in enumerate((t0, t1, t2, t3)):
        rows = place_of(x_ref[0], X - shift)
        products = dot(part[...], weights, 1, 1)
        outs[0][rows, :] = products[:, :COLS]
        for kind in range(1, SLOTS):
            outs[kind][rows, :] = products[:, kind * COLS : (kind + 1) * COLS].astype(BF16)


def tile_kernel(x_ref, t0, t1, t2, t3, tile_ref):
    for shift, part in enumerate((t0, t1, t2, t3)):
        tile_ref[place_of(x_ref[0], X - shift), :] = part[...]


def low_kernel(hidden_ref, sent_ref, factor_ref, other_ref, out_ref):
    factor = all_factor(factor_ref, other_ref)
    for part in range(X):
        rows = pl.ds(part * STEP, STEP)
        out_ref[rows, :] = hidden_ref[rows, :] + dot(sent_ref[rows, COLS:], factor, 1, 1)


def hidden_kernel(core_ref, hidden_ref, a, b, c, d, sent_ref, factor_ref, other_ref, dpre_ref, back_ref):
    factor = all_factor(factor_ref, other_ref)
    core = core_ref[0]
    for part in range(X):
        rows = pl.ds(part * STEP, STEP)
        hidden = hidden_ref[rows, :]
        for arrived in (a, b, c, d):
            hidden = hidden + arrived[rows, :].astype(F32)
        up = sent_ref[rows, :COLS].astype(F32)
        up = jnp.where(core == 0, up, pltpu.roll(up, OWN, 1))
        dpre = (up * gelu_slope(hidden)).astype(BF16)
        dpre_ref[rows, :] = dpre
        back_ref[rows, :] = dot(dpre, factor, 1, 0).astype(BF16)


def input_kernel(slot_ref, x_ref, a, b, c, d, e, mine_ref, other_ref, own_ref, *outs):
    weights = all_weights(slot_ref, mine_ref, other_ref)
    for shift in (2, 1, 3, 0):
        rows = place_of(x_ref[0], shift)
        stacked = jnp.concatenate([k[rows, :] for k in (a, b, c, d, e)], axis=1)
        result = dot(stacked, weights, 1, 0)
        if shift == 0:
            own_ref[...] = result
        else:
            outs[shift - 1][...] = result.astype(BF16)


def weight_kernel(slot_ref, a, b, c, d, e, tile_ref, sent_ref, keep_ref, away_ref, factor_ref):
    for kind, grads in enumerate((a, b, c, d, e)):
        slot = slot_ref[kind]
        full = dot(grads[...], tile_ref[...], 0, 0)
        keep_ref[slot] = full[:OWN]
        away_ref[pl.ds(pl.multiple_of(slot * OWN, OWN), OWN), :] = full[OWN:]
    full = dot(a[...], sent_ref[:, COLS:], 0, 0)
    factor_ref[...] = full[:OWN]
    away_ref[SLOTS * OWN :, :RANK] = full[OWN : OWN + OWN // 2]
    away_ref[SLOTS * OWN :, RANK:] = full[OWN + OWN // 2 :]


def code_kernel(tile_ref, back_ref, out_ref):
    out_ref[...] = dot(tile_ref[...], back_ref[...], 0, 0)


def body(inputs, block_weights, partners, code_in, code_out, upstream):
    core = lax.axis_index("c").reshape(1)
    place = lax.axis_index("x").reshape(1)
    row = lax.axis_index("h") * Z + lax.axis_index("z")
    own = (lax.axis_index("x") * Y + lax.axis_index("y")) * OWN
    inputs, core, place, row, own = lax.optimization_barrier((inputs, core, place, row, own))

    targets = jnp.bitwise_xor(row, jnp.array(MASKS, jnp.int32))
    slots = jnp.sum(
        jnp.where(partners[0][None, :] == targets[:, None], jnp.arange(SLOTS)[None, :], 0), axis=1
    ).astype(jnp.int32)

    factor = code_out[:, 0, :].T
    packed = jnp.concatenate([factor[: OWN // 2], factor[OWN // 2 :]], axis=1)
    mine = block_weights[0]
    other = swap_core(jnp.concatenate([mine.reshape(SLOTS * OWN, ROWS), packed], axis=0))

    near = spread(inputs, ("y",), Y).reshape(Y * OWN, ROWS)
    near = after(near, other)
    far = [to_x(near, shift) for shift in range(1, X)]

    codes = dot(inputs, code_in, 1, 0).astype(BF16)
    codes = spread(after(codes, near), ("h", "z"), H * Z)
    codes = codes.astype(F32).sum(0).astype(BF16)
    near = after(near, codes)

    tall = [shape((TOKENS, COLS), BF16)] * 4
    hidden, *terms = call(
        forward_kernel, [SMEM] * 2 + [VMEM] * 6,
        [shape((TOKENS, COLS), F32)] + tall,
        2 * TOKENS * COLS * SLOTS * ROWS, slots, place, near, *far, mine, other,
    )
    arrived = [from_partner(term, mask) for term, mask in zip(terms, MASKS[1:])]

    sent = upstream[0].T.reshape(OWN, PEERS, COLS).transpose(1, 0, 2)
    sent = jnp.concatenate([sent, jnp.broadcast_to(codes[None], (PEERS, OWN, RANK))], axis=2)
    sent = exchange(after(sent, hidden), ("x", "y")).reshape(TOKENS, COLS + RANK)
    (hidden,) = call(
        low_kernel, [VMEM] * 4, [shape((TOKENS, COLS), F32)],
        2 * TOKENS * COLS * RANK, hidden, sent, factor, other,
    )
    arrived = lax.optimization_barrier((hidden, *arrived))[1:]
    dpre, back = call(
        hidden_kernel, [SMEM] + [VMEM] * 8,
        [shape((TOKENS, COLS), BF16), shape((TOKENS, RANK), BF16)],
        2 * TOKENS * COLS * RANK, core, hidden, *arrived, sent, factor, other,
    )
    kinds = [dpre] + [from_partner(dpre, mask) for mask in MASKS[1:]]

    back = exchange(back.reshape(PEERS * H, OWN // H, RANK), ("x", "y", "h")).astype(F32).sum(0)

    back = back.astype(BF16)
    back = spread(back, ("z",), Z).astype(F32).sum(0).astype(BF16)
    kinds = lax.optimization_barrier((back, *kinds))[1:]
    back = spread(back, ("x", "y", "h"), PEERS * H).reshape(TOKENS, RANK)

    partial, *away = call(
        input_kernel, [SMEM] * 2 + [VMEM] * 7,
        [shape((STEP, ROWS), F32)] + [shape((STEP, ROWS), BF16)] * 3,
        2 * TOKENS * COLS * SLOTS * ROWS, slots, place, *kinds, mine, other,
    )
    came = [to_x(part, shift) for shift, part in enumerate(away, 1)]
    kinds = lax.optimization_barrier((*kinds, *came))[:SLOTS]
    near, *far = lax.optimization_barrier((near, *far, *came))[:X]
    (tile,) = call(
        tile_kernel, [SMEM] + [VMEM] * 4, [shape((TOKENS, ROWS), BF16)], 0, place, near, *far
    )
    for part in came:
        partial = partial + part.astype(F32)
    partial = after(partial, back)
    partial = exchange(partial.astype(BF16).reshape(Y, OWN, ROWS), ("y",))
    own_back = lax.dynamic_slice_in_dim(back, own, OWN, 0)
    input_grad = partial.astype(F32).sum(0) + dot(own_back, code_in, 1, 1)
    input_grad = input_grad.astype(BF16)

    keep, away, factor_grad = call(
        weight_kernel, [SMEM] + [VMEM] * 7,
        [shape((SLOTS, OWN, ROWS), F32), shape((SLOTS * OWN + OWN // 2, ROWS), F32), shape((OWN, RANK), F32)],
        2 * TOKENS * COLS * (SLOTS * ROWS + RANK), slots, *kinds, tile, sent,
    )
    came = swap_core(away)
    block_grad = keep + came[: SLOTS * OWN].reshape(SLOTS, OWN, ROWS)
    last = came[SLOTS * OWN :]
    factor_grad = factor_grad + jnp.concatenate([last[:, :RANK], last[:, RANK:]], axis=0)

    (code_in_grad,) = call(
        code_kernel, [VMEM] * 2, [shape((ROWS, RANK), F32)], 2 * TOKENS * ROWS * RANK, tile, back
    )
    code_in_grad = code_in_grad + swap_core(code_in_grad)

    return (input_grad, block_grad[None], code_in_grad, factor_grad.T[:, None, :])


def solution(mesh):
    fine = Mesh(mesh.devices.reshape(X, Y, C, H, Z), ("x", "y", "c", "h", "z"))
    dp, mp = ("x", "y", "c"), ("h", "z")
    in_specs = (
        P(dp, mp),
        P(mp, None, dp, None),
        P(mp, None),
        P(mp, None),
        P(None, mp, dp),
        P(mp, None, dp),
    )
    out_specs = (P(dp, mp), P(mp, None, dp, None), P(mp, None), P(None, mp, dp))
    return jax.shard_map(body, mesh=fine, in_specs=in_specs, out_specs=out_specs, check_vma=False)
```
